256 devices in a mesh: row: 16 (over z, x_lo), col: 16 (over y, x_hi, core).
Axes of the slice: x: 4 (x_hi: 2, x_lo: 2; x = x_hi * 2 + x_lo), y: 4, z: 8, core: 2. Of those that a mesh axis runs over, the one named last changes fastest.
Arguments:
- source_points: float32 [32, 32768], P(None, ('row', 'col')), may hold values from -16 to 16, as said below
- target_points: float32 [32, 32768], P(None, 'col'), may hold values from -16 to 16, as said below
- target_potential: float32 [32768], P('col'), may hold values from -3 to 3
Outputs:
- source_new: float32 [32768], P('row')
- target_new: float32 [32768], P('col')
- transport_map: float32 [32, 32768], P(None, ('row', 'col'))
- inverse_map: float32 [32, 32768], P(None, 'col')
The draws below stay inside these ranges and needn't reach their ends.
Inputs may be any that keep to these rules, and one draw needn't show every extreme that they name: `source_points`: each cell's coordinates are its own independent draws times a scale of that cell, clipped to the range. `target_points`: each cell's coordinates are its own independent draws times a scale of that cell, clipped to the range.
All inputs are finite; a program needn't handle non-finite values.
Results may differ from the reference program's by a relative error of at most 0.0003.
Values sent between devices are 32-bit elements; how exact they have to be, the bound alone decides.
No kernel may reach another device: no remote copies, remote signals or barrier semaphores. Data moves between devices by JAX's collectives and lax.ppermute only.
A program may use at most 64 MiB of HBM per device.

```python
import math
import jax
import jax.numpy as jnp
from jax import lax

DIM = 32
NS = 32768
NT = 32768


def cell_points(key, width, count):
    scale_key, value_key = jax.random.split(key)
    cell_scale = jnp.exp(jax.random.uniform(scale_key, (1, count), jnp.float32, jnp.log(0.25), jnp.log(16.0)))
    values = jax.random.truncated_normal(value_key, -4.0, 4.0, (width, count), jnp.float32)
    return jnp.clip(values * cell_scale, -16.0, 16.0)


def draw_source_points(key, part):
    key = jax.random.fold_in(key, 11)
    return cell_points(key, DIM, NS)


def draw_target_points(key, part):
    key = jax.random.fold_in(key, 23)
    return cell_points(key, DIM, NT)


def levels(rng, extent, pieces, low, top_value):
    def one(axis_at, parts):
        heights = jax.random.uniform(jax.random.fold_in(jax.random.fold_in(rng, 6), axis_at), (parts,), jnp.float32, low / len(pieces), top_value / len(pieces))
        return jnp.repeat(jnp.exp(heights), extent[axis_at] // parts).reshape((-1,) + (1,) * (len(extent) - axis_at - 1))

    gain = one(*pieces[0])
    for cut in pieces[1:]:
        gain = gain * one(*cut)
    return gain


def bell_draw(key, shape, scale, most, pieces=(), dtype=jnp.bfloat16):
    values = jax.random.normal(key, shape, jnp.float32) * scale
    if len(pieces) > 0:
        values = levels(key, shape, pieces, -0.22, 0.18) * values
    return jnp.clip(values, min=-most, max=most).astype(dtype)


def setup_inputs(seed: int = 0) -> dict:
    key_of = jax.random.split(jax.random.key(seed), 4)
    return {
        "source_points": draw_source_points(jax.random.fold_in(key_of[3], 71), 0),
        "target_points": draw_target_points(jax.random.fold_in(key_of[3], 71), 0),
        "target_potential": bell_draw(key_of[2], (NT,), 0.5, 3.0, ((0, 16),), jnp.float32),
    }


EPS = 0.05


def query_stats(queries, key_points, key_weight, want_mean, block_size):
    width = queries.shape[0]
    count = queries.shape[1]
    block_count = count // block_size
    query_sq = jnp.sum(queries * queries, axis=0)
    key_sq = jnp.sum(key_points * key_points, axis=0)
    blocked = jnp.transpose(queries.reshape(width, block_count, block_size), (1, 0, 2))
    blocked_sq = query_sq.reshape(block_count, block_size)

    def one_block(pair_in):
        query_block, query_norms = pair_in
        inner_term = jnp.dot(query_block.T, key_points, precision=lax.Precision.HIGHEST, preferred_element_type=jnp.float32)
        costs = (query_norms[:, None] + key_sq[None, :] - 2.0 * inner_term) / (2.0 * width)
        scores = (key_weight[None, :] - costs) / EPS
        peaks = jnp.max(scores, axis=1)
        expos = jnp.exp(scores - peaks[:, None])
        totals = jnp.sum(expos, axis=1)
        if want_mean:
            weighted = jnp.dot(expos, key_points.T, precision=lax.Precision.HIGHEST, preferred_element_type=jnp.float32)
        else:
            weighted = jnp.zeros((block_size, 1), jnp.float32)
        return peaks, totals, weighted

    peaks, totals, weighted = lax.map(one_block, (blocked, blocked_sq))
    peaks = peaks.reshape(count)
    totals = totals.reshape(count)
    weighted = weighted.reshape(count, weighted.shape[2]).T
    return peaks, totals, weighted


def reference(source_points, target_points, target_potential):
    block_rows = math.gcd(NS, 1024)
    block_cols = math.gcd(NT, 1024)
    peaks, totals, unused = query_stats(source_points, target_points, target_potential, False, block_rows)
    source_new = -EPS * math.log(NS) - EPS * (peaks + jnp.log(totals))
    peaks, totals, weighted = query_stats(target_points, source_points, source_new, True, block_cols)
    target_new = -EPS * math.log(NT) - EPS * (peaks + jnp.log(totals))
    inverse_map = weighted / totals[None, :]
    peaks, totals, weighted = query_stats(source_points, target_points, target_new, True, block_rows)
    transport_map = weighted / totals[None, :]
    return source_new, target_new, transport_map, inverse_map
```

```python
import functools
import math

import jax
import jax.numpy as jnp
from jax import lax
from jax.experimental import pallas as pl
from jax.experimental.pallas import tpu as pltpu
from jax.sharding import PartitionSpec as P

EPS = 0.05
F32 = jnp.float32
BF16 = jnp.bfloat16
LANES = 128
TILE = 256
LOG2E = math.log2(math.e)
VMEM_LIMIT = 48 * 1024 * 1024


def split(value, parts):
    out = []
    for _ in range(parts):
        part = value.astype(BF16)
        out.append(part)
        value = value - part.astype(F32)
    return out


def weight_rows(first, second):
    width = (first if first is not None else second).shape[1]
    row = lax.broadcasted_iota(jnp.int32, (16, width), 0)
    out = jnp.zeros((16, width), F32)
    for at, value in ((0, first), (3, second)):
        if value is None:
            out = jnp.where((row >= at) & (row < at + 3), 1.0, out)
        else:
            for k, part in enumerate(split(value, 3)):
                out = jnp.where(row == at + k, part.astype(F32), out)
    return out.astype(BF16)


def key_stack(points, weight):
    a, b, c = split(points, 3)
    return jnp.concatenate([a, b, a, c, a, b, weight_rows(weight, None)], axis=0)


def query_stack(points, weight):
    a, b, c = split(points, 3)
    zero = jnp.zeros((1, points.shape[1]), F32) if weight is None else weight
    return jnp.concatenate([a, a, b, a, c, b, weight_rows(None, zero)], axis=0)


def mean_rows(points):
    a, b, c = split(points, 3)
    ones = weight_rows(None, jnp.zeros((1, points.shape[1]), F32))
    keep = lax.broadcasted_iota(jnp.int32, ones.shape, 0) == 0
    ones = jnp.where(keep, ones.astype(F32), 0.0).astype(BF16)
    return jnp.concatenate([a, ones, b, c], axis=0)


def dot(a, b):
    return jnp.dot(a, b, preferred_element_type=F32)


def chunk_row(ref, chunks):
    return jnp.concatenate([ref[c] for c in range(chunks)], axis=1)


def peak8(scores):
    rows, cols = scores.shape
    return jnp.max(scores.reshape(rows // 8, 8, cols), axis=0)


def scores_tile(keys, queries, scores, slot, at):
    q = queries[:, pl.ds(pl.multiple_of(at * TILE, TILE), TILE)]
    peak = None
    for k in range(keys.shape[0] // TILE):
        s = dot(keys[k * TILE : (k + 1) * TILE, :], q)
        scores[slot, k * TILE : (k + 1) * TILE, :] = s
        p = peak8(s)
        peak = p if peak is None else jnp.maximum(peak, p)
    return jnp.max(peak, axis=0, keepdims=True)


def weighted(expos, means, k, sums):
    high = expos.astype(BF16)
    low = (expos - high.astype(F32)).astype(BF16)
    m = means[:, k * TILE : (k + 1) * TILE]
    full = dot(m, high)
    rest = dot(m[:80], low)
    part = full[:48] + rest[:48]
    tail = full[48:80] + full[80:112] + rest[48:80]
    return (part, tail) if sums is None else (sums[0] + part, sums[1] + tail)


def pipelined(steps, first, second):
    peak = first(0, 0)

    def step(at, peak):
        later = first(at, at % 2)
        second(at - 1, (at - 1) % 2, peak)
        return later

    peak = lax.fori_loop(1, steps, step, peak)
    second(steps - 1, (steps - 1) % 2, peak)


def forward_kernel(scale, x_ref, y_ref, g_ref, out_ref, keys, queries, scores):
    count = y_ref.shape[1]
    y = y_ref[...]
    weight = g_ref[...] * (LOG2E / EPS) - scale * jnp.sum(y * y, axis=0, keepdims=True)
    keys[...] = key_stack(y, weight).T
    chunks = x_ref.shape[0]
    queries[...] = query_stack(chunk_row(x_ref, chunks) * (2.0 * scale), None)

    def first(at, slot):
        return scores_tile(keys, queries, scores, slot, at)

    def second(at, slot, peak):
        total = None
        for k in range(count // TILE):
            e = jnp.exp2(scores[slot, k * TILE : (k + 1) * TILE, :] - peak)
            t = jnp.sum(e.reshape(TILE // 8, 8, TILE), axis=0)
            total = t if total is None else total + t
        total = jnp.sum(total, axis=0, keepdims=True)
        pair = jnp.concatenate([peak, total], axis=0)
        lanes = pl.ds(pl.multiple_of(at * TILE, TILE), TILE)
        for c in range(out_ref.shape[0]):
            out_ref[c, :, lanes] = pair

    pipelined(queries.shape[1] // TILE, first, second)


def backward_kernel(scale, total_count, x_ref, y_ref, stats_ref, out_ref, f_ref, h_ref, keys, queries, scores, means, lse):
    chunks = x_ref.shape[0]
    x = chunk_row(x_ref, chunks)
    peaks = stats_ref[:, 0, :]
    top = jnp.max(peaks, axis=0, keepdims=True)
    total = jnp.sum(stats_ref[:, 1, :] * jnp.exp2(peaks - top), axis=0, keepdims=True)
    h = -math.log2(total_count) - (top + jnp.log2(total))
    h_ref[...] = h
    f_ref[...] = (EPS / LOG2E) * (h + scale * jnp.sum(x * x, axis=0, keepdims=True))
    keys[...] = key_stack(x, h).T
    queries[...] = query_stack(y_ref[...] * (2.0 * scale), None)
    means[...] = mean_rows(x)

    def first(at, slot):
        return scores_tile(keys, queries, scores, slot, at)

    def second(at, slot, peak):
        sums = None
        for k in range(keys.shape[0] // TILE):
            e = jnp.exp2(scores[slot, k * TILE : (k + 1) * TILE, :] - peak)
            sums = weighted(e, means, k, sums)
        total = sums[0][32:33]
        mean = (sums[0][:32] + sums[1]) / total
        value = peak + jnp.log2(total)
        for c in range(TILE // LANES):
            cut = slice(c * LANES, (c + 1) * LANES)
            out_ref[at * (TILE // LANES) + c, :32, :] = mean[:, cut]
            lse[pl.ds(at * (TILE // LANES) + c, 1), :] = value[:, cut]

    pipelined(queries.shape[1] // TILE, first, second)
    rows = lse[...]
    for c in range(out_ref.shape[0]):
        out_ref[c, 32:, :] = rows


def reduce_kernel(in_ref, out_ref, lse_ref):
    me = lax.axis_index("row")
    every = in_ref[:, 32:, :]
    top = jnp.max(every, axis=0)
    lse_ref[...] = top + jnp.log2(jnp.sum(jnp.exp2(every - top[None]), axis=0))
    mine = in_ref[:, pl.ds(32 + me, 1), :]
    share = jnp.exp2(mine - lse_ref[pl.ds(me, 1), :][None])
    value = jnp.sum(in_ref[:, :32, :] * share, axis=0)
    for c in range(out_ref.shape[0]):
        out_ref[c] = value


def plan_kernel(scale, total_count, x_ref, y_ref, h_ref, lse_ref, out_ref, g_ref, keys, queries, means):
    y = y_ref[...]
    lse = jnp.concatenate([lse_ref[c : c + 1, :] for c in range(lse_ref.shape[0])], axis=1)
    y_sq = jnp.sum(y * y, axis=0, keepdims=True)
    g_ref[...] = (EPS / LOG2E) * (scale * y_sq - math.log2(total_count) - lse)
    keys[...] = key_stack(y, -lse).T
    chunks = x_ref.shape[0]
    queries[...] = query_stack(chunk_row(x_ref, chunks) * (2.0 * scale), h_ref[...])
    means[...] = mean_rows(y)

    def step(at, carry):
        q = queries[:, pl.ds(pl.multiple_of(at * TILE, TILE), TILE)]
        sums = None
        for k in range(keys.shape[0] // TILE):
            e = jnp.exp2(dot(keys[k * TILE : (k + 1) * TILE, :], q))
            sums = weighted(e, means, k, sums)
        for c in range(TILE // LANES):
            cut = slice(c * LANES, (c + 1) * LANES)
            out_ref[at * (TILE // LANES) + c, :32, :] = sums[0][:32, cut] + sums[1][:, cut]
            out_ref[at * (TILE // LANES) + c, 32:, :] = sums[0][32:40, cut]
        return carry

    lax.fori_loop(0, queries.shape[1] // TILE, step, 0)


def finish_kernel(in_ref, inv_ref, out_ref, inv_out_ref):
    sums = jnp.sum(in_ref[...], axis=0)
    out_ref[...] = sums[:32] / sums[32:33]
    for c in range(inv_ref.shape[0]):
        inv_out_ref[:, c * LANES : (c + 1) * LANES] = inv_ref[c]


def call(body, outs, scratch, flops, *args):
    return pl.pallas_call(
        body,
        out_shape=[jax.ShapeDtypeStruct(s, F32) for s in outs],
        in_specs=[pl.BlockSpec(memory_space=pltpu.VMEM)] * len(args),
        out_specs=[pl.BlockSpec(memory_space=pltpu.VMEM)] * len(outs),
        scratch_shapes=scratch,
        compiler_params=pltpu.CompilerParams(vmem_limit_bytes=VMEM_LIMIT),
        cost_estimate=pl.CostEstimate(flops=flops, bytes_accessed=1 << 20, transcendentals=0),
    )(*args)


def local(source_points, target_points, target_potential):
    width, own = source_points.shape
    cols, rows = lax.axis_size("col"), lax.axis_size("row")
    n, m = own * cols, target_points.shape[1]
    source_count, target_count = n * rows, m * cols
    scale = LOG2E / (2.0 * width * EPS)
    depth = 6 * width + 16
    keys = pltpu.VMEM((m, depth), BF16)
    queries = pltpu.VMEM((depth, n), BF16)
    scores = pltpu.VMEM((2, m, TILE), F32)
    means = pltpu.VMEM((3 * width + 16, m), BF16)
    flops = 2 * n * m * 256

    x = lax.all_to_all(jnp.broadcast_to(source_points, (cols, width, own)), "col", 0, 0)
    (stats,) = call(
        functools.partial(forward_kernel, scale),
        [(cols, 2, n)],
        [keys, queries, scores],
        flops,
        x,
        target_points,
        target_potential.reshape(1, m),
    )
    stats = lax.all_to_all(stats, "col", 0, 0)
    partial, f, h = call(
        functools.partial(backward_kernel, scale, target_count),
        [(rows, width + rows, m // rows), (1, n), (1, n)],
        [keys, queries, scores, means, pltpu.VMEM((rows, m // rows), F32)],
        2 * flops,
        x,
        target_points,
        stats,
    )
    partial = lax.all_to_all(partial, "row", 0, 0)
    inverse, lse = call(reduce_kernel, [(rows, width, m // rows), (rows, m // rows)], [], 1 << 20, partial)
    inverse = lax.all_to_all(inverse, "row", 0, 0)
    plan, g = call(
        functools.partial(plan_kernel, scale, source_count),
        [(cols, width + 8, own), (1, m)],
        [keys, queries, means],
        2 * flops,
        x,
        target_points,
        h,
        lse,
    )
    plan = lax.all_to_all(plan, "col", 0, 0)
    transport_map, inverse_map = call(finish_kernel, [(width, own), (width, m)], [], 1 << 20, plan, inverse)
    return f.reshape(n), g.reshape(m), transport_map, inverse_map


def solution(mesh):
    in_specs = (P(None, ("row", "col")), P(None, "col"), P("col"))
    out_specs = (P("row"), P("col"), P(None, ("row", "col")), P(None, "col"))
    return jax.shard_map(local, mesh=mesh, in_specs=in_specs, out_specs=out_specs, check_vma=False)
```

```python
import functools
import math

import jax
import jax.numpy as jnp
from jax import lax
from jax.experimental import pallas as pl
from jax.experimental.pallas import tpu as pltpu
from jax.sharding import PartitionSpec as P

EPS = 0.05
F32 = jnp.float32
BF16 = jnp.bfloat16
LANES = 128
TILE = 256
BLOCK = 512
LOG2E = math.log2(math.e)
VMEM_LIMIT = 48 * 1024 * 1024


def split(value, parts):
    out = []
    for _ in range(parts):
        part = value.astype(BF16)
        out.append(part)
        value = value - part.astype(F32)
    return out


def weight_rows(first, second):
    width = (first if first is not None else second).shape[1]
    row = lax.broadcasted_iota(jnp.int32, (16, width), 0)
    out = jnp.zeros((16, width), F32)
    for at, value in ((0, first), (3, second)):
        if value is None:
            out = jnp.where((row >= at) & (row < at + 3), 1.0, out)
        else:
            for k, part in enumerate(split(value, 3)):
                out = jnp.where(row == at + k, part.astype(F32), out)
    return out.astype(BF16)


def key_stack(points, weight):
    a, b, c = split(points, 3)
    return jnp.concatenate([a, b, a, c, a, b, weight_rows(weight, None)], axis=0)


def query_stack(points, weight):
    a, b, c = split(points, 3)
    zero = jnp.zeros((1, points.shape[1]), F32) if weight is None else weight
    return jnp.concatenate([a, a, b, a, c, b, weight_rows(None, zero)], axis=0)


def mean_rows(points):
    a, b, c = split(points, 3)
    ones = weight_rows(None, jnp.zeros((1, points.shape[1]), F32))
    keep = lax.broadcasted_iota(jnp.int32, ones.shape, 0) == 0
    ones = jnp.where(keep, ones.astype(F32), 0.0).astype(BF16)
    return jnp.concatenate([a, ones, b, c], axis=0)


def dot(a, b):
    return jnp.dot(a, b, preferred_element_type=F32)


def chunk_row(ref, chunks):
    return jnp.concatenate([ref[c] for c in range(chunks)], axis=1)


def peak8(scores):
    rows, cols = scores.shape
    return jnp.max(scores.reshape(rows // 8, 8, cols), axis=0)


def scores_tile(keys, queries, scores, at):
    q = queries[:, at * TILE : (at + 1) * TILE]
    peak = None
    for k in range(keys.shape[0] // BLOCK):
        s = dot(keys[k * BLOCK : (k + 1) * BLOCK, :], q)
        scores[at % 2, k * BLOCK : (k + 1) * BLOCK, :] = s
        p = peak8(s)
        peak = p if peak is None else jnp.maximum(peak, p)
    return jnp.max(peak, axis=0, keepdims=True)


def weighted(expos, means, k, sums):
    high = expos.astype(BF16)
    low = (expos - high.astype(F32)).astype(BF16)
    m = means[:, k * BLOCK : (k + 1) * BLOCK]
    full = dot(m, high)
    rest = dot(m[:80], low)
    part = full[:48] + rest[:48]
    tail = full[48:80] + full[80:112] + rest[48:80]
    return (part, tail) if sums is None else (sums[0] + part, sums[1] + tail)


def pipelined(steps, first, second):
    peak = first(0)
    for at in range(steps):
        later = first(at + 1) if at + 1 < steps else None
        second(at, peak)
        peak = later


def forward_kernel(scale, x_ref, y_ref, g_ref, out_ref, keys, queries, scores):
    count = y_ref.shape[1]
    y = y_ref[...]
    weight = g_ref[...] * (LOG2E / EPS) - scale * jnp.sum(y * y, axis=0, keepdims=True)
    keys[...] = key_stack(y, weight).T
    chunks = x_ref.shape[0]
    queries[...] = query_stack(chunk_row(x_ref, chunks) * (2.0 * scale), None)

    def first(at):
        return scores_tile(keys, queries, scores, at)

    def second(at, peak):
        total = None
        for k in range(count // BLOCK):
            e = jnp.exp2(scores[at % 2, k * BLOCK : (k + 1) * BLOCK, :] - peak)
            t = jnp.sum(e.reshape(BLOCK // 8, 8, TILE), axis=0)
            total = t if total is None else total + t
        total = jnp.sum(total, axis=0, keepdims=True)
        pair = jnp.concatenate([peak, total], axis=0)
        for c in range(out_ref.shape[0]):
            out_ref[c, :, at * TILE : (at + 1) * TILE] = pair

    pipelined(queries.shape[1] // TILE, first, second)


def backward_kernel(scale, total_count, x_ref, y_ref, stats_ref, out_ref, f_ref, h_ref, keys, queries, scores, means):
    chunks = x_ref.shape[0]
    x = chunk_row(x_ref, chunks)
    peaks = stats_ref[:, 0, :]
    top = jnp.max(peaks, axis=0, keepdims=True)
    total = jnp.sum(stats_ref[:, 1, :] * jnp.exp2(peaks - top), axis=0, keepdims=True)
    h = -math.log2(total_count) - (top + jnp.log2(total))
    h_ref[...] = h
    f_ref[...] = (EPS / LOG2E) * (h + scale * jnp.sum(x * x, axis=0, keepdims=True))
    keys[...] = key_stack(x, h).T
    queries[...] = query_stack(y_ref[...] * (2.0 * scale), None)
    means[...] = mean_rows(x)

    def first(at):
        return scores_tile(keys, queries, scores, at)

    def second(at, peak):
        sums = None
        for k in range(keys.shape[0] // BLOCK):
            e = jnp.exp2(scores[at % 2, k * BLOCK : (k + 1) * BLOCK, :] - peak)
            sums = weighted(e, means, k, sums)
        total = sums[0][32:33]
        mean = (sums[0][:32] + sums[1]) / total
        value = jnp.broadcast_to(peak + jnp.log2(total), (8, TILE))
        for c in range(TILE // LANES):
            cut = slice(c * LANES, (c + 1) * LANES)
            out_ref[at * (TILE // LANES) + c, :32, :] = mean[:, cut]
            out_ref[at * (TILE // LANES) + c, 32:, :] = value[:, cut]

    pipelined(queries.shape[1] // TILE, first, second)


def reduce_kernel(in_ref, out_ref):
    every = in_ref[:, 32:, :]
    top = jnp.max(every, axis=0)
    lse = top + jnp.log2(jnp.sum(jnp.exp2(every - top[None]), axis=0))
    share = jnp.exp2(every - lse[None])[:, :1, :]
    value = jnp.sum(in_ref[:, :32, :] * share, axis=0)
    for c in range(out_ref.shape[0]):
        out_ref[c, :32, :] = value
        out_ref[c, 32:, :] = lse


def plan_kernel(scale, total_count, x_ref, y_ref, h_ref, in_ref, out_ref, g_ref, inv_ref, keys, queries, means):
    y = y_ref[...]
    lse = jnp.concatenate([in_ref[c, 32:33, :] for c in range(in_ref.shape[0])], axis=1)
    y_sq = jnp.sum(y * y, axis=0, keepdims=True)
    g_ref[...] = (EPS / LOG2E) * (scale * y_sq - math.log2(total_count) - lse)
    keys[...] = key_stack(y, -lse).T
    chunks = x_ref.shape[0]
    queries[...] = query_stack(chunk_row(x_ref, chunks) * (2.0 * scale), h_ref[...])
    means[...] = mean_rows(y)
    for c in range(in_ref.shape[0]):
        inv_ref[:, c * LANES : (c + 1) * LANES] = in_ref[c, :32, :]

    for at in range(queries.shape[1] // TILE):
        q = queries[:, at * TILE : (at + 1) * TILE]
        sums = None
        for k in range(keys.shape[0] // BLOCK):
            e = jnp.exp2(dot(keys[k * BLOCK : (k + 1) * BLOCK, :], q))
            sums = weighted(e, means, k, sums)
        for c in range(TILE // LANES):
            cut = slice(c * LANES, (c + 1) * LANES)
            out_ref[at * (TILE // LANES) + c, :32, :] = sums[0][:32, cut] + sums[1][:, cut]
            out_ref[at * (TILE // LANES) + c, 32:, :] = sums[0][32:40, cut]


def finish_kernel(in_ref, out_ref):
    sums = jnp.sum(in_ref[...], axis=0)
    out_ref[...] = sums[:32] / sums[32:33]


def call(body, outs, scratch, flops, *args):
    return pl.pallas_call(
        body,
        out_shape=[jax.ShapeDtypeStruct(s, F32) for s in outs],
        in_specs=[pl.BlockSpec(memory_space=pltpu.VMEM)] * len(args),
        out_specs=[pl.BlockSpec(memory_space=pltpu.VMEM)] * len(outs),
        scratch_shapes=scratch,
        compiler_params=pltpu.CompilerParams(vmem_limit_bytes=VMEM_LIMIT),
        cost_estimate=pl.CostEstimate(flops=flops, bytes_accessed=1 << 20, transcendentals=0),
    )(*args)


def local(source_points, target_points, target_potential):
    width, own = source_points.shape
    cols, rows = lax.axis_size("col"), lax.axis_size("row")
    n, m = own * cols, target_points.shape[1]
    source_count, target_count = n * rows, m * cols
    scale = LOG2E / (2.0 * width * EPS)
    depth = 6 * width + 16
    keys = pltpu.VMEM((m, depth), BF16)
    queries = pltpu.VMEM((depth, n), BF16)
    scores = pltpu.VMEM((2, m, TILE), F32)
    means = pltpu.VMEM((3 * width + 16, m), BF16)
    flops = 2 * n * m * 256

    x = lax.all_to_all(jnp.broadcast_to(source_points, (cols, width, own)), "col", 0, 0)
    (stats,) = call(
        functools.partial(forward_kernel, scale),
        [(cols, 2, n)],
        [keys, queries, scores],
        flops,
        x,
        target_points,
        target_potential.reshape(1, m),
    )
    stats = lax.all_to_all(stats, "col", 0, 0)
    partial, f, h = call(
        functools.partial(backward_kernel, scale, target_count),
        [(rows, width + 8, m // rows), (1, n), (1, n)],
        [keys, queries, scores, means],
        2 * flops,
        x,
        target_points,
        stats,
    )
    partial = lax.all_to_all(partial, "row", 0, 0)
    (both,) = call(reduce_kernel, [(rows, width + 8, m // rows)], [], 1 << 20, partial)
    both = lax.all_to_all(both, "row", 0, 0)
    plan, g, inverse_map = call(
        functools.partial(plan_kernel, scale, source_count),
        [(cols, width + 8, own), (1, m), (width, m)],
        [keys, queries, means],
        2 * flops,
        x,
        target_points,
        h,
        both,
    )
    plan = lax.all_to_all(plan, "col", 0, 0)
    (transport_map,) = call(finish_kernel, [(width, own)], [], 1 << 20, plan)
    return f.reshape(n), g.reshape(m), transport_map, inverse_map


def solution(mesh):
    in_specs = (P(None, ("row", "col")), P(None, "col"), P("col"))
    out_specs = (P("row"), P("col"), P(None, ("row", "col")), P(None, "col"))
    return jax.shard_map(local, mesh=mesh, in_specs=in_specs, out_specs=out_specs, check_vma=False)
```

```python
import functools
import math

import jax
import jax.numpy as jnp
from jax import lax
from jax.experimental import pallas as pl
from jax.experimental.pallas import tpu as pltpu
from jax.sharding import PartitionSpec as P

EPS = 0.05
F32 = jnp.float32
BF16 = jnp.bfloat16
LANES = 128
TILE = 256
BLOCK = 512
LOG2E = math.log2(math.e)
VMEM_LIMIT = 48 * 1024 * 1024


def split(value, parts):
    out = []
    for _ in range(parts):
        part = value.astype(BF16)
        out.append(part)
        value = value - part.astype(F32)
    return out


def weight_rows(first, second):
    width = (first if first is not None else second).shape[1]
    row = lax.broadcasted_iota(jnp.int32, (16, width), 0)
    out = jnp.zeros((16, width), F32)
    for at, value in ((0, first), (3, second)):
        if value is None:
            out = jnp.where((row >= at) & (row < at + 3), 1.0, out)
        else:
            for k, part in enumerate(split(value, 3)):
                out = jnp.where(row == at + k, part.astype(F32), out)
    return out.astype(BF16)


def key_stack(points, weight):
    a, b, c = split(points, 3)
    return jnp.concatenate([a, b, a, c, a, b, weight_rows(weight, None)], axis=0)


def query_stack(points, weight):
    a, b, c = split(points, 3)
    zero = jnp.zeros((1, points.shape[1]), F32) if weight is None else weight
    return jnp.concatenate([a, a, b, a, c, b, weight_rows(None, zero)], axis=0)


def mean_rows(points):
    a, b, c = split(points, 3)
    ones = weight_rows(None, jnp.zeros((1, points.shape[1]), F32))
    keep = lax.broadcasted_iota(jnp.int32, ones.shape, 0) == 0
    ones = jnp.where(keep, ones.astype(F32), 0.0).astype(BF16)
    return jnp.concatenate([a, ones, b, c], axis=0)


def dot(a, b):
    return jnp.dot(a, b, preferred_element_type=F32)


def chunk_row(ref, chunks):
    return jnp.concatenate([ref[c] for c in range(chunks)], axis=1)


def peak8(scores):
    rows, cols = scores.shape
    return jnp.max(scores.reshape(rows // 8, 8, cols), axis=0)


def scores_tile(keys, queries, scores, at):
    q = queries[:, at * TILE : (at + 1) * TILE]
    peak = None
    for k in range(keys.shape[0] // BLOCK):
        s = dot(keys[k * BLOCK : (k + 1) * BLOCK, :], q)
        scores[at % 2, k * BLOCK : (k + 1) * BLOCK, :] = s
        p = peak8(s)
        peak = p if peak is None else jnp.maximum(peak, p)
    return jnp.max(peak, axis=0, keepdims=True)


def weighted(expos, means, k, sums):
    high = expos.astype(BF16)
    low = (expos - high.astype(F32)).astype(BF16)
    m = means[:, k * BLOCK : (k + 1) * BLOCK]
    full = dot(m, high)
    rest = dot(m[:80], low)
    part = full[:48] + rest[:48]
    tail = full[48:80] + full[80:112] + rest[48:80]
    return (part, tail) if sums is None else (sums[0] + part, sums[1] + tail)


def pipelined(steps, first, second):
    peak = first(0)
    for at in range(steps):
        later = first(at + 1) if at + 1 < steps else None
        second(at, peak)
        peak = later


def forward_kernel(scale, x_ref, y_ref, g_ref, out_ref, keys, queries, scores):
    count = y_ref.shape[1]
    y = y_ref[...]
    weight = g_ref[...] * (LOG2E / EPS) - scale * jnp.sum(y * y, axis=0, keepdims=True)
    keys[...] = key_stack(y, weight).T
    chunks = x_ref.shape[0]
    queries[...] = query_stack(chunk_row(x_ref, chunks) * (2.0 * scale), None)

    def first(at):
        return scores_tile(keys, queries, scores, at)

    def second(at, peak):
        total = None
        for k in range(count // BLOCK):
            e = jnp.exp2(scores[at % 2, k * BLOCK : (k + 1) * BLOCK, :] - peak)
            t = jnp.sum(e.reshape(BLOCK // 8, 8, TILE), axis=0)
            total = t if total is None else total + t
        total = jnp.sum(total, axis=0, keepdims=True)
        pair = jnp.concatenate([peak, total], axis=0)
        for c in range(out_ref.shape[0]):
            out_ref[c, :, at * TILE : (at + 1) * TILE] = pair

    pipelined(queries.shape[1] // TILE, first, second)


def backward_kernel(scale, total_count, x_ref, y_ref, stats_ref, out_ref, f_ref, h_ref, keys, queries, scores, means, lse):
    chunks = x_ref.shape[0]
    x = chunk_row(x_ref, chunks)
    peaks = stats_ref[:, 0, :]
    top = jnp.max(peaks, axis=0, keepdims=True)
    total = jnp.sum(stats_ref[:, 1, :] * jnp.exp2(peaks - top), axis=0, keepdims=True)
    h = -math.log2(total_count) - (top + jnp.log2(total))
    h_ref[...] = h
    f_ref[...] = (EPS / LOG2E) * (h + scale * jnp.sum(x * x, axis=0, keepdims=True))
    keys[...] = key_stack(x, h).T
    queries[...] = query_stack(y_ref[...] * (2.0 * scale), None)
    means[...] = mean_rows(x)

    def first(at):
        return scores_tile(keys, queries, scores, at)

    def second(at, peak):
        sums = None
        for k in range(keys.shape[0] // BLOCK):
            e = jnp.exp2(scores[at % 2, k * BLOCK : (k + 1) * BLOCK, :] - peak)
            sums = weighted(e, means, k, sums)
        total = sums[0][32:33]
        mean = (sums[0][:32] + sums[1]) / total
        value = peak + jnp.log2(total)
        for c in range(TILE // LANES):
            cut = slice(c * LANES, (c + 1) * LANES)
            to = at * (TILE // LANES) + c
            out_ref[to, :32, :] = mean[:, cut]
            lse[to : to + 1, :] = value[:, cut]

    pipelined(queries.shape[1] // TILE, first, second)
    rows = lse[...]
    for c in range(out_ref.shape[0]):
        out_ref[c, 32:, :] = rows


def reduce_kernel(in_ref, out_ref, lse_ref):
    me = lax.axis_index("row")
    every = in_ref[:, 32:, :]
    top = jnp.max(every, axis=0)
    lse_ref[...] = top + jnp.log2(jnp.sum(jnp.exp2(every - top[None]), axis=0))
    mine = in_ref[:, pl.ds(32 + me, 1), :]
    share = jnp.exp2(mine - lse_ref[pl.ds(me, 1), :][None])
    value = jnp.sum(in_ref[:, :32, :] * share, axis=0)
    for c in range(out_ref.shape[0]):
        out_ref[c] = value


def plan_kernel(scale, total_count, x_ref, y_ref, h_ref, lse_ref, out_ref, g_ref, keys, queries, means):
    y = y_ref[...]
    lse = jnp.concatenate([lse_ref[c : c + 1, :] for c in range(lse_ref.shape[0])], axis=1)
    y_sq = jnp.sum(y * y, axis=0, keepdims=True)
    g_ref[...] = (EPS / LOG2E) * (scale * y_sq - math.log2(total_count) - lse)
    keys[...] = key_stack(y, -lse).T
    chunks = x_ref.shape[0]
    queries[...] = query_stack(chunk_row(x_ref, chunks) * (2.0 * scale), h_ref[...])
    means[...] = mean_rows(y)

    for at in range(queries.shape[1] // TILE):
        q = queries[:, at * TILE : (at + 1) * TILE]
        sums = None
        for k in range(keys.shape[0] // BLOCK):
            e = jnp.exp2(dot(keys[k * BLOCK : (k + 1) * BLOCK, :], q))
            sums = weighted(e, means, k, sums)
        for c in range(TILE // LANES):
            cut = slice(c * LANES, (c + 1) * LANES)
            out_ref[at * (TILE // LANES) + c, :32, :] = sums[0][:32, cut] + sums[1][:, cut]
            out_ref[at * (TILE // LANES) + c, 32:, :] = sums[0][32:40, cut]


def finish_kernel(in_ref, inv_ref, out_ref, inv_out_ref):
    sums = jnp.sum(in_ref[...], axis=0)
    out_ref[...] = sums[:32] / sums[32:33]
    for c in range(inv_ref.shape[0]):
        inv_out_ref[:, c * LANES : (c + 1) * LANES] = inv_ref[c]


def call(body, outs, scratch, flops, *args):
    return pl.pallas_call(
        body,
        out_shape=[jax.ShapeDtypeStruct(s, F32) for s in outs],
        in_specs=[pl.BlockSpec(memory_space=pltpu.VMEM)] * len(args),
        out_specs=[pl.BlockSpec(memory_space=pltpu.VMEM)] * len(outs),
        scratch_shapes=scratch,
        compiler_params=pltpu.CompilerParams(vmem_limit_bytes=VMEM_LIMIT),
        cost_estimate=pl.CostEstimate(flops=flops, bytes_accessed=1 << 20, transcendentals=0),
    )(*args)


def local(source_points, target_points, target_potential):
    width, own = source_points.shape
    cols, rows = lax.axis_size("col"), lax.axis_size("row")
    n, m = own * cols, target_points.shape[1]
    source_count, target_count = n * rows, m * cols
    scale = LOG2E / (2.0 * width * EPS)
    depth = 6 * width + 16
    keys = pltpu.VMEM((m, depth), BF16)
    queries = pltpu.VMEM((depth, n), BF16)
    scores = pltpu.VMEM((2, m, TILE), F32)
    means = pltpu.VMEM((3 * width + 16, m), BF16)
    flops = 2 * n * m * 256

    x = lax.all_to_all(jnp.broadcast_to(source_points, (cols, width, own)), "col", 0, 0)
    (stats,) = call(
        functools.partial(forward_kernel, scale),
        [(cols, 2, n)],
        [keys, queries, scores],
        flops,
        x,
        target_points,
        target_potential.reshape(1, m),
    )
    stats = lax.all_to_all(stats, "col", 0, 0)
    partial, f, h = call(
        functools.partial(backward_kernel, scale, target_count),
        [(rows, width + rows, m // rows), (1, n), (1, n)],
        [keys, queries, scores, means, pltpu.VMEM((rows, m // rows), F32)],
        2 * flops,
        x,
        target_points,
        stats,
    )
    partial = lax.all_to_all(partial, "row", 0, 0)
    inverse, lse = call(reduce_kernel, [(rows, width, m // rows), (rows, m // rows)], [], 1 << 20, partial)
    inverse = lax.all_to_all(inverse, "row", 0, 0)
    plan, g = call(
        functools.partial(plan_kernel, scale, source_count),
        [(cols, width + 8, own), (1, m)],
        [keys, queries, means],
        2 * flops,
        x,
        target_points,
        h,
        lse,
    )
    plan, inverse = lax.optimization_barrier((plan, inverse))
    plan = lax.all_to_all(plan, "col", 0, 0)
    transport_map, inverse_map = call(finish_kernel, [(width, own), (width, m)], [], 1 << 20, plan, inverse)
    return f.reshape(n), g.reshape(m), transport_map, inverse_map


def solution(mesh):
    in_specs = (P(None, ("row", "col")), P(None, "col"), P("col"))
    out_specs = (P("row"), P("col"), P(None, ("row", "col")), P(None, "col"))
    return jax.shard_map(local, mesh=mesh, in_specs=in_specs, out_specs=out_specs, check_vma=False)
```

```python
import functools
import math
import operator

import jax
import jax.numpy as jnp
from jax import lax
from jax.experimental import pallas as pl
from jax.experimental.pallas import tpu as pltpu
from jax.sharding import PartitionSpec as P

EPS = 0.05
F32 = jnp.float32
BF16 = jnp.bfloat16
LANES = 128
TILE = 256
BLOCK = 512
SMALL = 256
HOPS = (1, -2, 3)
LOG2E = math.log2(math.e)
VMEM_LIMIT = 48 * 1024 * 1024


def split(value, parts):
    out = []
    for _ in range(parts):
        part = value.astype(BF16)
        out.append(part)
        value = value - part.astype(F32)
    return out


def weight_rows(first, second):
    width = (first if first is not None else second).shape[1]
    row = lax.broadcasted_iota(jnp.int32, (16, width), 0)
    out = jnp.zeros((16, width), F32)
    for at, value in ((0, first), (3, second)):
        if value is None:
            out = jnp.where((row >= at) & (row < at + 3), 1.0, out)
        else:
            for k, part in enumerate(split(value, 3)):
                out = jnp.where(row == at + k, part.astype(F32), out)
    return out.astype(BF16)


def key_stack(points, weight):
    a, b, c = split(points, 3)
    return jnp.concatenate([a, b, a, c, a, b, weight_rows(weight, None)], axis=0)


def query_stack(points, weight):
    a, b, c = split(points, 3)
    zero = jnp.zeros((1, points.shape[1]), F32) if weight is None else weight
    return jnp.concatenate([a, a, b, a, c, b, weight_rows(None, zero)], axis=0)


def mean_rows(points):
    a, b = split(points, 2)
    ones = weight_rows(None, jnp.zeros((1, points.shape[1]), F32))
    keep = lax.broadcasted_iota(jnp.int32, ones.shape, 0) == 0
    ones = jnp.where(keep, ones.astype(F32), 0.0).astype(BF16)
    return jnp.concatenate([b, a, ones], axis=0)


def dot(a, b):
    return jnp.dot(a, b, preferred_element_type=F32)


def chunk_row(ref, chunks):
    return jnp.concatenate([ref[c] for c in range(chunks)], axis=1)


def peak8(scores):
    rows, cols = scores.shape
    return jnp.max(scores.reshape(rows // 8, 8, cols), axis=0)


def weighted(expos, means, k):
    high = expos.astype(BF16)
    low = (expos - high.astype(F32)).astype(BF16)
    m = means[:, k * BLOCK : (k + 1) * BLOCK]
    return [dot(m, high), dot(m[32:], low)]


def joined(sums):
    full, rest = sums
    return full[:32] + full[32:64] + rest[:32], full[64:72] + rest[32:40]


def forward_kernel(scale, x_ref, y_ref, g_ref, out_ref, keys, queries):
    count = y_ref.shape[1]
    y = y_ref[...]
    weight = g_ref[...] * (LOG2E / EPS) - scale * jnp.sum(y * y, axis=0, keepdims=True)
    keys[...] = key_stack(y, weight).T
    chunks = x_ref.shape[0]
    queries[...] = query_stack(chunk_row(x_ref, chunks) * (2.0 * scale), None)

    for at in range(queries.shape[1] // TILE):
        q = queries[:, at * TILE : (at + 1) * TILE]
        peak, total = None, None
        for k in range(count // SMALL):
            s = dot(keys[k * SMALL : (k + 1) * SMALL, :], q).reshape(SMALL // 8, 8, TILE)
            top = jnp.max(s, axis=0)
            later = top if peak is None else jnp.maximum(peak, top)
            t = jnp.sum(jnp.exp2(s - later[None]), axis=0)
            total = t if total is None else total * jnp.exp2(peak - later) + t
            peak = later
        top = jnp.max(peak, axis=0, keepdims=True)
        total = jnp.sum(total * jnp.exp2(peak - top), axis=0, keepdims=True)
        pair = jnp.concatenate([top, total], axis=0)
        for c in range(out_ref.shape[0]):
            out_ref[c, :, at * TILE : (at + 1) * TILE] = pair


def backward_kernel(scale, total_count, x_ref, y_ref, stats_ref, out_ref, f_ref, h_ref, keys, queries, means, lse):
    chunks = x_ref.shape[0]
    x = chunk_row(x_ref, chunks)
    peaks = stats_ref[:, 0, :]
    top = jnp.max(peaks, axis=0, keepdims=True)
    total = jnp.sum(stats_ref[:, 1, :] * jnp.exp2(peaks - top), axis=0, keepdims=True)
    h = -math.log2(total_count) - (top + jnp.log2(total))
    h_ref[...] = h
    f_ref[...] = (EPS / LOG2E) * (h + scale * jnp.sum(x * x, axis=0, keepdims=True))
    keys[...] = key_stack(x, h).T
    queries[...] = query_stack(y_ref[...] * (2.0 * scale), None)
    means[...] = mean_rows(x)

    for at in range(queries.shape[1] // TILE):
        q = queries[:, at * TILE : (at + 1) * TILE]
        peak, sums = None, None
        for k in range(keys.shape[0] // BLOCK):
            s = dot(keys[k * BLOCK : (k + 1) * BLOCK, :], q)
            top = jnp.max(peak8(s), axis=0, keepdims=True)
            later = top if peak is None else jnp.maximum(peak, top)
            part = weighted(jnp.exp2(s - later), means, k)
            if sums is None:
                sums = part
            else:
                factor = jnp.exp2(peak - later)
                sums = [old * factor + new for old, new in zip(sums, part)]
            peak = later
        mean, total = joined(sums)
        mean, total = mean / total[:1], total[:1]
        value = peak + jnp.log2(total)
        for c in range(TILE // LANES):
            cut = slice(c * LANES, (c + 1) * LANES)
            to = at * (TILE // LANES) + c
            out_ref[to, :32, :] = mean[:, cut]
            lse[to : to + 1, :] = value[:, cut]

    rows = lse[...]
    for c in range(out_ref.shape[0]):
        out_ref[c, 32:, :] = rows


def reduce_kernel(in_ref, out_ref, lse_ref):
    me = lax.axis_index("row")
    every = in_ref[:, 32:, :]
    top = jnp.max(every, axis=0)
    lse_ref[...] = top + jnp.log2(jnp.sum(jnp.exp2(every - top[None]), axis=0))
    mine = in_ref[:, pl.ds(32 + me, 1), :]
    share = jnp.exp2(mine - lse_ref[pl.ds(me, 1), :][None])
    out_ref[...] = jnp.sum(in_ref[:, :32, :] * share, axis=0)


def plan_kernel(scale, total_count, x_ref, y_ref, h_ref, lse_ref, out_ref, g_ref, keys, queries, means):
    y = y_ref[...]
    lse = jnp.concatenate([lse_ref[c : c + 1, :] for c in range(lse_ref.shape[0])], axis=1)
    y_sq = jnp.sum(y * y, axis=0, keepdims=True)
    g_ref[...] = (EPS / LOG2E) * (scale * y_sq - math.log2(total_count) - lse)
    keys[...] = key_stack(y, -lse).T
    chunks = x_ref.shape[0]
    queries[...] = query_stack(chunk_row(x_ref, chunks) * (2.0 * scale), h_ref[...])
    means[...] = mean_rows(y)

    for at in range(queries.shape[1] // TILE):
        q = queries[:, at * TILE : (at + 1) * TILE]
        sums = None
        for k in range(keys.shape[0] // BLOCK):
            e = jnp.exp2(dot(keys[k * BLOCK : (k + 1) * BLOCK, :], q))
            part = weighted(e, means, k)
            sums = part if sums is None else [old + new for old, new in zip(sums, part)]
        mean, total = joined(sums)
        for c in range(TILE // LANES):
            cut = slice(c * LANES, (c + 1) * LANES)
            out_ref[at * (TILE // LANES) + c, :32, :] = mean[:, cut]
            out_ref[at * (TILE // LANES) + c, 32:, :] = total[:, cut]


def outward(hop, z):
    return z + hop if z % 2 == 1 else z - hop


def from_rows(value, rows, level, side):
    levels = rows // 2
    return lax.ppermute(value, "row", [(level(r // 2) % levels * 2 + (r % 2 ^ side), r) for r in range(rows)])


def finish_kernel(in_ref, *refs):
    pieces, (out_ref, inv_ref) = refs[:-2], refs[-2:]
    sums = jnp.sum(in_ref[...], axis=0)
    out_ref[...] = sums[:32] / sums[32:33]
    me = lax.axis_index("row")
    levels = inv_ref.shape[1] // LANES // 2
    level, side = me // 2, me % 2
    sign = 2 * (level % 2) - 1
    for ref, hop in zip(pieces, (0,) + HOPS):
        source = lax.rem(level + sign * hop + levels, levels)
        mate = source + 1 - 2 * (source % 2)
        for at in range(4):
            chunk = (source if at < 2 else mate) * 2 + (side if at % 2 == 0 else 1 - side)
            inv_ref[:, pl.ds(pl.multiple_of(chunk * LANES, LANES), LANES)] = ref[at * 32 : (at + 1) * 32, :]


def call(body, outs, scratch, flops, *args):
    return pl.pallas_call(
        body,
        out_shape=[jax.ShapeDtypeStruct(s, F32) for s in outs],
        in_specs=[pl.BlockSpec(memory_space=pltpu.VMEM)] * len(args),
        out_specs=[pl.BlockSpec(memory_space=pltpu.VMEM)] * len(outs),
        scratch_shapes=scratch,
        compiler_params=pltpu.CompilerParams(vmem_limit_bytes=VMEM_LIMIT),
        cost_estimate=pl.CostEstimate(flops=flops, bytes_accessed=1 << 20, transcendentals=0),
    )(*args)


def local(source_points, target_points, target_potential):
    width, own = source_points.shape
    cols, rows = lax.axis_size("col"), lax.axis_size("row")
    n, m = own * cols, target_points.shape[1]
    source_count, target_count = n * rows, m * cols
    scale = LOG2E / (2.0 * width * EPS)
    depth = 6 * width + 16
    keys = pltpu.VMEM((m, depth), BF16)
    queries = pltpu.VMEM((depth, n), BF16)
    means = pltpu.VMEM((2 * width + 16, m), BF16)
    flops = 2 * n * m * 256

    x = lax.all_to_all(jnp.broadcast_to(source_points, (cols, width, own)), "col", 0, 0)
    (stats,) = call(
        functools.partial(forward_kernel, scale),
        [(cols, 2, n)],
        [keys, queries],
        flops,
        x,
        target_points,
        target_potential.reshape(1, m),
    )
    stats = lax.all_to_all(stats, "col", 0, 0)
    partial, f, h = call(
        functools.partial(backward_kernel, scale, target_count),
        [(rows, width + rows, m // rows), (1, n), (1, n)],
        [keys, queries, means, pltpu.VMEM((rows, m // rows), F32)],
        2 * flops,
        x,
        target_points,
        stats,
    )
    partial = lax.all_to_all(partial, "row", 0, 0)
    inverse, lse = call(reduce_kernel, [(width, m // rows), (rows, m // rows)], [], 1 << 20, partial)
    pieces = [inverse] + [from_rows(inverse, rows, functools.partial(operator.xor, level), side) for level, side in ((0, 1), (1, 0), (1, 1))]
    four = jnp.concatenate(pieces, axis=0)
    pieces = [four] + [from_rows(four, rows, functools.partial(outward, hop), 0) for hop in HOPS]
    plan, g = call(
        functools.partial(plan_kernel, scale, source_count),
        [(cols, width + 8, own), (1, m)],
        [keys, queries, means],
        2 * flops,
        x,
        target_points,
        h,
        lse,
    )
    plan = lax.all_to_all(plan, "col", 0, 0)
    transport_map, inverse_map = call(finish_kernel, [(width, own), (width, m)], [], 1 << 20, plan, *pieces)
    return f.reshape(n), g.reshape(m), transport_map, inverse_map


def solution(mesh):
    in_specs = (P(None, ("row", "col")), P(None, "col"), P("col"))
    out_specs = (P("row"), P("col"), P(None, ("row", "col")), P(None, "col"))
    return jax.shard_map(local, mesh=mesh, in_specs=in_specs, out_specs=out_specs, check_vma=False)
```

```python
import functools
import math
import operator

import jax
import jax.numpy as jnp
from jax import lax
from jax.experimental import pallas as pl
from jax.experimental.pallas import tpu as pltpu
from jax.sharding import PartitionSpec as P

EPS = 0.05
F32 = jnp.float32
BF16 = jnp.bfloat16
LANES = 128
TILE = 256
BLOCK = 512
SMALL = 256
HOPS = (1, -2, 3)
LOG2E = math.log2(math.e)
VMEM_LIMIT = 48 * 1024 * 1024


def split(value, parts):
    out = []
    for _ in range(parts):
        part = value.astype(BF16)
        out.append(part)
        value = value - part.astype(F32)
    return out


def weight_rows(first, second):
    width = (first if first is not None else second).shape[1]
    row = lax.broadcasted_iota(jnp.int32, (16, width), 0)
    out = jnp.zeros((16, width), F32)
    for at, value in ((0, first), (3, second)):
        if value is None:
            out = jnp.where((row >= at) & (row < at + 3), 1.0, out)
        else:
            for k, part in enumerate(split(value, 3)):
                out = jnp.where(row == at + k, part.astype(F32), out)
    return out.astype(BF16)


def key_stack(points, weight):
    a, b, c = split(points, 3)
    return jnp.concatenate([a, b, a, c, a, b, weight_rows(weight, None)], axis=0)


def query_stack(points, weight):
    a, b, c = split(points, 3)
    zero = jnp.zeros((1, points.shape[1]), F32) if weight is None else weight
    return jnp.concatenate([a, a, b, a, c, b, weight_rows(None, zero)], axis=0)


def mean_rows(points):
    a, b, c = split(points, 3)
    ones = weight_rows(None, jnp.zeros((1, points.shape[1]), F32))
    keep = lax.broadcasted_iota(jnp.int32, ones.shape, 0) == 0
    ones = jnp.where(keep, ones.astype(F32), 0.0).astype(BF16)
    return jnp.concatenate([a, ones, b, c], axis=0)


def dot(a, b):
    return jnp.dot(a, b, preferred_element_type=F32)


def chunk_row(ref, chunks):
    return jnp.concatenate([ref[c] for c in range(chunks)], axis=1)


def peak8(scores):
    rows, cols = scores.shape
    return jnp.max(scores.reshape(rows // 8, 8, cols), axis=0)


def weighted(expos, means, k):
    high = expos.astype(BF16)
    low = (expos - high.astype(F32)).astype(BF16)
    m = means[:, k * BLOCK : (k + 1) * BLOCK]
    full, rest = dot(m, high), dot(m[:80], low)
    return [full[:48] + rest[:48], full[48:80] + full[80:112] + rest[48:80]]


def joined(sums):
    part, tail = sums
    return part[:32] + tail, part[32:40]


def forward_kernel(scale, x_ref, y_ref, g_ref, out_ref, keys, queries):
    count = y_ref.shape[1]
    y = y_ref[...]
    weight = g_ref[...] * (LOG2E / EPS) - scale * jnp.sum(y * y, axis=0, keepdims=True)
    keys[...] = key_stack(y, weight).T
    chunks = x_ref.shape[0]
    queries[...] = query_stack(chunk_row(x_ref, chunks) * (2.0 * scale), None)

    for at in range(queries.shape[1] // TILE):
        q = queries[:, at * TILE : (at + 1) * TILE]
        peak, total = None, None
        for k in range(count // SMALL):
            s = dot(keys[k * SMALL : (k + 1) * SMALL, :], q).reshape(SMALL // 8, 8, TILE)
            top = jnp.max(s, axis=0)
            later = top if peak is None else jnp.maximum(peak, top)
            t = jnp.sum(jnp.exp2(s - later[None]), axis=0)
            total = t if total is None else total * jnp.exp2(peak - later) + t
            peak = later
        top = jnp.max(peak, axis=0, keepdims=True)
        total = jnp.sum(total * jnp.exp2(peak - top), axis=0, keepdims=True)
        pair = jnp.concatenate([top, total], axis=0)
        for c in range(out_ref.shape[0]):
            out_ref[c, :, at * TILE : (at + 1) * TILE] = pair


def backward_kernel(scale, total_count, x_ref, y_ref, stats_ref, out_ref, h_ref, keys, queries, means, lse):
    chunks = x_ref.shape[0]
    x = chunk_row(x_ref, chunks)
    peaks = stats_ref[:, 0, :]
    top = jnp.max(peaks, axis=0, keepdims=True)
    total = jnp.sum(stats_ref[:, 1, :] * jnp.exp2(peaks - top), axis=0, keepdims=True)
    h = -math.log2(total_count) - (top + jnp.log2(total))
    h_ref[...] = h
    keys[...] = key_stack(x, h).T
    queries[...] = query_stack(y_ref[...] * (2.0 * scale), None)
    means[...] = mean_rows(x)

    for at in range(queries.shape[1] // TILE):
        q = queries[:, at * TILE : (at + 1) * TILE]
        peak, sums = None, None
        for k in range(keys.shape[0] // BLOCK):
            s = dot(keys[k * BLOCK : (k + 1) * BLOCK, :], q)
            top = jnp.max(peak8(s), axis=0, keepdims=True)
            later = top if peak is None else jnp.maximum(peak, top)
            part = weighted(jnp.exp2(s - later), means, k)
            if sums is None:
                sums = part
            else:
                factor = jnp.exp2(peak - later)
                sums = [old * factor + new for old, new in zip(sums, part)]
            peak = later
        mean, total = joined(sums)
        mean, total = mean / total[:1], total[:1]
        value = peak + jnp.log2(total)
        for c in range(TILE // LANES):
            cut = slice(c * LANES, (c + 1) * LANES)
            to = at * (TILE // LANES) + c
            out_ref[to, :32, :] = mean[:, cut]
            lse[to : to + 1, :] = value[:, cut]

    rows = lse[...]
    for c in range(out_ref.shape[0]):
        out_ref[c, 32:, :] = rows


def reduce_kernel(in_ref, out_ref, lse_ref):
    me = lax.axis_index("row")
    every = in_ref[:, 32:, :]
    top = jnp.max(every, axis=0)
    lse_ref[...] = top + jnp.log2(jnp.sum(jnp.exp2(every - top[None]), axis=0))
    mine = in_ref[:, pl.ds(32 + me, 1), :]
    share = jnp.exp2(mine - lse_ref[pl.ds(me, 1), :][None])
    out_ref[...] = jnp.sum(in_ref[:, :32, :] * share, axis=0)


def plan_kernel(scale, x_ref, y_ref, h_ref, lse_ref, out_ref, keys, queries, means):
    y = y_ref[...]
    lse = jnp.concatenate([lse_ref[c : c + 1, :] for c in range(lse_ref.shape[0])], axis=1)
    keys[...] = key_stack(y, -lse).T
    chunks = x_ref.shape[0]
    queries[...] = query_stack(chunk_row(x_ref, chunks) * (2.0 * scale), h_ref[...])
    means[...] = mean_rows(y)

    for at in range(queries.shape[1] // TILE):
        q = queries[:, at * TILE : (at + 1) * TILE]
        sums = None
        for k in range(keys.shape[0] // BLOCK):
            e = jnp.exp2(dot(keys[k * BLOCK : (k + 1) * BLOCK, :], q))
            part = weighted(e, means, k)
            sums = part if sums is None else [old + new for old, new in zip(sums, part)]
        mean, total = joined(sums)
        for c in range(TILE // LANES):
            cut = slice(c * LANES, (c + 1) * LANES)
            out_ref[at * (TILE // LANES) + c, :32, :] = mean[:, cut]
            out_ref[at * (TILE // LANES) + c, 32:, :] = total[:, cut]


def outward(hop, z):
    return z + hop if z % 2 == 1 else z - hop


def from_rows(value, rows, level, side):
    levels = rows // 2
    return lax.ppermute(value, "row", [(level(r // 2) % levels * 2 + (r % 2 ^ side), r) for r in range(rows)])


def potentials_kernel(scale, total_count, x_ref, y_ref, h_ref, lse_ref, f_ref, g_ref):
    x, y = chunk_row(x_ref, x_ref.shape[0]), y_ref[...]
    lse = jnp.concatenate([lse_ref[c : c + 1, :] for c in range(lse_ref.shape[0])], axis=1)
    x_sq = jnp.sum(x * x, axis=0, keepdims=True)
    y_sq = jnp.sum(y * y, axis=0, keepdims=True)
    f_ref[...] = (EPS / LOG2E) * (h_ref[...] + scale * x_sq)
    g_ref[...] = (EPS / LOG2E) * (scale * y_sq - math.log2(total_count) - lse)


def finish_kernel(in_ref, *refs):
    pieces, (out_ref, inv_ref) = refs[:-2], refs[-2:]
    sums = jnp.sum(in_ref[...], axis=0)
    out_ref[...] = sums[:32] / sums[32:33]
    me = lax.axis_index("row")
    levels = inv_ref.shape[1] // LANES // 2
    level, side = me // 2, me % 2
    sign = 2 * (level % 2) - 1
    for ref, hop in zip(pieces, (0,) + HOPS):
        source = lax.rem(level + sign * hop + levels, levels)
        mate = source + 1 - 2 * (source % 2)
        for at in range(4):
            chunk = (source if at < 2 else mate) * 2 + (side if at % 2 == 0 else 1 - side)
            inv_ref[:, pl.ds(pl.multiple_of(chunk * LANES, LANES), LANES)] = ref[at * 32 : (at + 1) * 32, :]


def call(body, outs, scratch, flops, *args):
    return pl.pallas_call(
        body,
        out_shape=[jax.ShapeDtypeStruct(s, F32) for s in outs],
        in_specs=[pl.BlockSpec(memory_space=pltpu.VMEM)] * len(args),
        out_specs=[pl.BlockSpec(memory_space=pltpu.VMEM)] * len(outs),
        scratch_shapes=scratch,
        compiler_params=pltpu.CompilerParams(vmem_limit_bytes=VMEM_LIMIT),
        cost_estimate=pl.CostEstimate(flops=flops, bytes_accessed=1 << 20, transcendentals=0),
    )(*args)


def local(source_points, target_points, target_potential):
    width, own = source_points.shape
    cols, rows = lax.axis_size("col"), lax.axis_size("row")
    n, m = own * cols, target_points.shape[1]
    source_count, target_count = n * rows, m * cols
    scale = LOG2E / (2.0 * width * EPS)
    depth = 6 * width + 16
    keys = pltpu.VMEM((m, depth), BF16)
    queries = pltpu.VMEM((depth, n), BF16)
    means = pltpu.VMEM((3 * width + 16, m), BF16)
    flops = 2 * n * m * 256

    x = lax.all_to_all(jnp.broadcast_to(source_points, (cols, width, own)), "col", 0, 0)
    (stats,) = call(
        functools.partial(forward_kernel, scale),
        [(cols, 2, n)],
        [keys, queries],
        flops,
        x,
        target_points,
        target_potential.reshape(1, m),
    )
    stats = lax.all_to_all(stats, "col", 0, 0)
    partial, h = call(
        functools.partial(backward_kernel, scale, target_count),
        [(rows, width + rows, m // rows), (1, n)],
        [keys, queries, means, pltpu.VMEM((rows, m // rows), F32)],
        2 * flops,
        x,
        target_points,
        stats,
    )
    partial = lax.all_to_all(partial, "row", 0, 0)
    inverse, lse = call(reduce_kernel, [(width, m // rows), (rows, m // rows)], [], 1 << 20, partial)
    pieces = [inverse] + [from_rows(inverse, rows, functools.partial(operator.xor, level), side) for level, side in ((0, 1), (1, 0), (1, 1))]
    four = jnp.concatenate(pieces, axis=0)
    pieces = [four] + [from_rows(four, rows, functools.partial(outward, hop), 0) for hop in HOPS]
    (plan,) = call(
        functools.partial(plan_kernel, scale),
        [(cols, width + 8, own)],
        [keys, queries, means],
        2 * flops,
        x,
        target_points,
        h,
        lse,
    )
    plan, h, lse = lax.optimization_barrier((plan, h, lse))
    plan = lax.all_to_all(plan, "col", 0, 0)
    f, g = call(
        functools.partial(potentials_kernel, scale, source_count),
        [(1, n), (1, m)],
        [],
        1 << 20,
        x,
        target_points,
        h,
        lse,
    )
    transport_map, inverse_map = call(finish_kernel, [(width, own), (width, m)], [], 1 << 20, plan, *pieces)
    return f.reshape(n), g.reshape(m), transport_map, inverse_map


def solution(mesh):
    in_specs = (P(None, ("row", "col")), P(None, "col"), P("col"))
    out_specs = (P("row"), P("col"), P(None, ("row", "col")), P(None, "col"))
    return jax.shard_map(local, mesh=mesh, in_specs=in_specs, out_specs=out_specs, check_vma=False)
```

```python
import functools
import math
import operator

import jax
import jax.numpy as jnp
from jax import lax
from jax.experimental import pallas as pl
from jax.experimental.pallas import tpu as pltpu
from jax.sharding import PartitionSpec as P

EPS = 0.05
F32 = jnp.float32
BF16 = jnp.bfloat16
LANES = 128
TILE = 256
BLOCK = 512
SMALL = 256
HOPS = (-2, 1, 3)
LOG2E = math.log2(math.e)
VMEM_LIMIT = 48 * 1024 * 1024


def split(value, parts):
    out = []
    for _ in range(parts):
        part = value.astype(BF16)
        out.append(part)
        value = value - part.astype(F32)
    return out


def weight_rows(first, second):
    width = (first if first is not None else second).shape[1]
    row = lax.broadcasted_iota(jnp.int32, (16, width), 0)
    out = jnp.zeros((16, width), F32)
    for at, value in ((0, first), (3, second)):
        if value is None:
            out = jnp.where((row >= at) & (row < at + 3), 1.0, out)
        else:
            for k, part in enumerate(split(value, 3)):
                out = jnp.where(row == at + k, part.astype(F32), out)
    return out.astype(BF16)


def key_stack(points, weight):
    a, b, c = split(points, 3)
    return jnp.concatenate([a, b, a, c, a, b, weight_rows(weight, None)], axis=0)


def query_stack(points, weight):
    a, b, c = split(points, 3)
    zero = jnp.zeros((1, points.shape[1]), F32) if weight is None else weight
    return jnp.concatenate([a, a, b, a, c, b, weight_rows(None, zero)], axis=0)


def mean_rows(points):
    a, b, c = split(points, 3)
    ones = weight_rows(None, jnp.zeros((1, points.shape[1]), F32))
    keep = lax.broadcasted_iota(jnp.int32, ones.shape, 0) == 0
    ones = jnp.where(keep, ones.astype(F32), 0.0).astype(BF16)
    return jnp.concatenate([a, ones, b, c], axis=0)


def dot(a, b):
    return jnp.dot(a, b, preferred_element_type=F32)


def chunk_row(ref, chunks):
    return jnp.concatenate([ref[c] for c in range(chunks)], axis=1)


def peak8(scores):
    rows, cols = scores.shape
    return jnp.max(scores.reshape(rows // 8, 8, cols), axis=0)


def weighted(expos, means, k):
    high = expos.astype(BF16)
    low = (expos - high.astype(F32)).astype(BF16)
    m = means[:, k * BLOCK : (k + 1) * BLOCK]
    full, rest = dot(m, high), dot(m[:80], low)
    return [full[:48] + rest[:48], full[48:80] + full[80:112] + rest[48:80]]


def joined(sums):
    part, tail = sums
    return part[:32] + tail, part[32:40]


def forward_kernel(scale, x_ref, y_ref, g_ref, out_ref, keys, queries):
    count = y_ref.shape[1]
    y = y_ref[...]
    weight = g_ref[...] * (LOG2E / EPS) - scale * jnp.sum(y * y, axis=0, keepdims=True)
    keys[...] = key_stack(y, weight).T
    chunks = x_ref.shape[0]
    queries[...] = query_stack(chunk_row(x_ref, chunks) * (2.0 * scale), None)

    for at in range(queries.shape[1] // TILE):
        q = queries[:, at * TILE : (at + 1) * TILE]
        peak, total = None, None
        for k in range(count // SMALL):
            s = dot(keys[k * SMALL : (k + 1) * SMALL, :], q).reshape(SMALL // 8, 8, TILE)
            top = jnp.max(s, axis=0)
            later = top if peak is None else jnp.maximum(peak, top)
            t = jnp.sum(jnp.exp2(s - later[None]), axis=0)
            total = t if total is None else total * jnp.exp2(peak - later) + t
            peak = later
        top = jnp.max(peak, axis=0, keepdims=True)
        total = jnp.sum(total * jnp.exp2(peak - top), axis=0, keepdims=True)
        pair = jnp.concatenate([top, total], axis=0)
        for c in range(out_ref.shape[0]):
            out_ref[c, :, at * TILE : (at + 1) * TILE] = pair


def backward_kernel(scale, total_count, x_ref, y_ref, stats_ref, out_ref, h_ref, keys, queries, means, lse):
    chunks = x_ref.shape[0]
    x = chunk_row(x_ref, chunks)
    peaks = stats_ref[:, 0, :]
    top = jnp.max(peaks, axis=0, keepdims=True)
    total = jnp.sum(stats_ref[:, 1, :] * jnp.exp2(peaks - top), axis=0, keepdims=True)
    h = -math.log2(total_count) - (top + jnp.log2(total))
    h_ref[...] = h
    keys[...] = key_stack(x, h).T
    queries[...] = query_stack(y_ref[...] * (2.0 * scale), None)
    means[...] = mean_rows(x)

    for at in range(queries.shape[1] // TILE):
        q = queries[:, at * TILE : (at + 1) * TILE]
        peak, sums = None, None
        for k in range(keys.shape[0] // BLOCK):
            s = dot(keys[k * BLOCK : (k + 1) * BLOCK, :], q)
            top = jnp.max(peak8(s), axis=0, keepdims=True)
            later = top if peak is None else jnp.maximum(peak, top)
            part = weighted(jnp.exp2(s - later), means, k)
            if sums is None:
                sums = part
            else:
                factor = jnp.exp2(peak - later)
                sums = [old * factor + new for old, new in zip(sums, part)]
            peak = later
        mean, total = joined(sums)
        mean, total = mean / total[:1], total[:1]
        value = peak + jnp.log2(total)
        for c in range(TILE // LANES):
            cut = slice(c * LANES, (c + 1) * LANES)
            to = at * (TILE // LANES) + c
            out_ref[to, :32, :] = mean[:, cut]
            lse[to : to + 1, :] = value[:, cut]

    rows = lse[...]
    for c in range(out_ref.shape[0]):
        out_ref[c, 32:, :] = rows


def reduce_kernel(in_ref, out_ref, lse_ref):
    me = lax.axis_index("row")
    every = in_ref[:, 32:, :]
    top = jnp.max(every, axis=0)
    lse_ref[...] = top + jnp.log2(jnp.sum(jnp.exp2(every - top[None]), axis=0))
    mine = in_ref[:, pl.ds(32 + me, 1), :]
    share = jnp.exp2(mine - lse_ref[pl.ds(me, 1), :][None])
    out_ref[...] = jnp.sum(in_ref[:, :32, :] * share, axis=0)


def plan_kernel(scale, x_ref, y_ref, h_ref, lse_ref, out_ref, keys, queries, means):
    y = y_ref[...]
    lse = jnp.concatenate([lse_ref[c : c + 1, :] for c in range(lse_ref.shape[0])], axis=1)
    keys[...] = key_stack(y, -lse).T
    chunks = x_ref.shape[0]
    queries[...] = query_stack(chunk_row(x_ref, chunks) * (2.0 * scale), h_ref[...])
    means[...] = mean_rows(y)

    for at in range(queries.shape[1] // TILE):
        q = queries[:, at * TILE : (at + 1) * TILE]
        sums = None
        for k in range(keys.shape[0] // BLOCK):
            e = jnp.exp2(dot(keys[k * BLOCK : (k + 1) * BLOCK, :], q))
            part = weighted(e, means, k)
            sums = part if sums is None else [old + new for old, new in zip(sums, part)]
        mean, total = joined(sums)
        for c in range(TILE // LANES):
            cut = slice(c * LANES, (c + 1) * LANES)
            out_ref[at * (TILE // LANES) + c, :32, :] = mean[:, cut]
            out_ref[at * (TILE // LANES) + c, 32:, :] = total[:, cut]


def outward(hop, z):
    return z + hop if z % 2 == 1 else z - hop


def from_rows(value, rows, level, side):
    levels = rows // 2
    return lax.ppermute(value, "row", [(level(r // 2) % levels * 2 + (r % 2 ^ side), r) for r in range(rows)])


def potentials_kernel(scale, total_count, x_ref, y_ref, h_ref, lse_ref, f_ref, g_ref):
    x, y = chunk_row(x_ref, x_ref.shape[0]), y_ref[...]
    lse = jnp.concatenate([lse_ref[c : c + 1, :] for c in range(lse_ref.shape[0])], axis=1)
    x_sq = jnp.sum(x * x, axis=0, keepdims=True)
    y_sq = jnp.sum(y * y, axis=0, keepdims=True)
    f_ref[...] = (EPS / LOG2E) * (h_ref[...] + scale * x_sq)
    g_ref[...] = (EPS / LOG2E) * (scale * y_sq - math.log2(total_count) - lse)


def finish_kernel(in_ref, *refs):
    pieces, (out_ref, inv_ref) = refs[:-2], refs[-2:]
    sums = jnp.sum(in_ref[...], axis=0)
    out_ref[...] = sums[:32] / sums[32:33]
    me = lax.axis_index("row")
    levels = inv_ref.shape[1] // LANES // 2
    level, side = me // 2, me % 2
    sign = 2 * (level % 2) - 1
    for ref, hop in zip(pieces, (0,) + HOPS):
        source = lax.rem(level + sign * hop + levels, levels)
        mate = source + 1 - 2 * (source % 2)
        for at in range(4):
            chunk = (source if at < 2 else mate) * 2 + (side if at % 2 == 0 else 1 - side)
            inv_ref[:, pl.ds(pl.multiple_of(chunk * LANES, LANES), LANES)] = ref[at * 32 : (at + 1) * 32, :]


def call(body, outs, scratch, flops, *args):
    return pl.pallas_call(
        body,
        out_shape=[jax.ShapeDtypeStruct(s, F32) for s in outs],
        in_specs=[pl.BlockSpec(memory_space=pltpu.VMEM)] * len(args),
        out_specs=[pl.BlockSpec(memory_space=pltpu.VMEM)] * len(outs),
        scratch_shapes=scratch,
        compiler_params=pltpu.CompilerParams(vmem_limit_bytes=VMEM_LIMIT),
        cost_estimate=pl.CostEstimate(flops=flops, bytes_accessed=1 << 20, transcendentals=0),
    )(*args)


def local(source_points, target_points, target_potential):
    width, own = source_points.shape
    cols, rows = lax.axis_size("col"), lax.axis_size("row")
    n, m = own * cols, target_points.shape[1]
    source_count, target_count = n * rows, m * cols
    scale = LOG2E / (2.0 * width * EPS)
    depth = 6 * width + 16
    keys = pltpu.VMEM((m, depth), BF16)
    queries = pltpu.VMEM((depth, n), BF16)
    means = pltpu.VMEM((3 * width + 16, m), BF16)
    flops = 2 * n * m * 256

    x = lax.all_to_all(jnp.broadcast_to(source_points, (cols, width, own)), "col", 0, 0)
    (stats,) = call(
        functools.partial(forward_kernel, scale),
        [(cols, 2, n)],
        [keys, queries],
        flops,
        x,
        target_points,
        target_potential.reshape(1, m),
    )
    stats = lax.all_to_all(stats, "col", 0, 0)
    partial, h = call(
        functools.partial(backward_kernel, scale, target_count),
        [(rows, width + rows, m // rows), (1, n)],
        [keys, queries, means, pltpu.VMEM((rows, m // rows), F32)],
        2 * flops,
        x,
        target_points,
        stats,
    )
    partial = lax.all_to_all(partial, "row", 0, 0)
    inverse, lse = call(reduce_kernel, [(width, m // rows), (rows, m // rows)], [], 1 << 20, partial)
    pieces = [inverse] + [from_rows(inverse, rows, functools.partial(operator.xor, level), side) for level, side in ((0, 1), (1, 0), (1, 1))]
    four = jnp.concatenate(pieces, axis=0)
    pieces = [four] + [from_rows(four, rows, functools.partial(outward, hop), 0) for hop in HOPS]
    (plan,) = call(
        functools.partial(plan_kernel, scale),
        [(cols, width + 8, own)],
        [keys, queries, means],
        2 * flops,
        x,
        target_points,
        h,
        lse,
    )
    plan, h, lse = lax.optimization_barrier((plan, h, lse))
    plan = lax.all_to_all(plan, "col", 0, 0)
    f, g = call(
        functools.partial(potentials_kernel, scale, source_count),
        [(1, n), (1, m)],
        [],
        1 << 20,
        x,
        target_points,
        h,
        lse,
    )
    transport_map, inverse_map = call(finish_kernel, [(width, own), (width, m)], [], 1 << 20, plan, *pieces)
    return f.reshape(n), g.reshape(m), transport_map, inverse_map


def solution(mesh):
    in_specs = (P(None, ("row", "col")), P(None, "col"), P("col"))
    out_specs = (P("row"), P("col"), P(None, ("row", "col")), P(None, "col"))
    return jax.shard_map(local, mesh=mesh, in_specs=in_specs, out_specs=out_specs, check_vma=False)
```

```python
import functools
import math
import operator

import jax
import jax.numpy as jnp
from jax import lax
from jax.experimental import pallas as pl
from jax.experimental.pallas import tpu as pltpu
from jax.sharding import PartitionSpec as P

EPS = 0.05
F32 = jnp.float32
BF16 = jnp.bfloat16
LANES = 128
TILE = 256
BLOCK = 512
SMALL = 128
HOPS = (-2, 1, 3)
LOG2E = math.log2(math.e)
VMEM_LIMIT = 48 * 1024 * 1024


def split(value, parts):
    out = []
    for _ in range(parts):
        part = value.astype(BF16)
        out.append(part)
        value = value - part.astype(F32)
    return out


def weight_rows(first, second):
    width = (first if first is not None else second).shape[1]
    row = lax.broadcasted_iota(jnp.int32, (16, width), 0)
    out = jnp.zeros((16, width), F32)
    for at, value in ((0, first), (3, second)):
        if value is None:
            out = jnp.where((row >= at) & (row < at + 3), 1.0, out)
        else:
            for k, part in enumerate(split(value, 3)):
                out = jnp.where(row == at + k, part.astype(F32), out)
    return out.astype(BF16)


def key_stack(points, weight):
    a, b, c = split(points, 3)
    return jnp.concatenate([a, b, a, c, a, b, weight_rows(weight, None)], axis=0)


def query_stack(points, weight):
    a, b, c = split(points, 3)
    zero = jnp.zeros((1, points.shape[1]), F32) if weight is None else weight
    return jnp.concatenate([a, a, b, a, c, b, weight_rows(None, zero)], axis=0)


def mean_rows(points):
    a, b, c = split(points, 3)
    ones = weight_rows(None, jnp.zeros((1, points.shape[1]), F32))
    keep = lax.broadcasted_iota(jnp.int32, ones.shape, 0) == 0
    ones = jnp.where(keep, ones.astype(F32), 0.0).astype(BF16)
    return jnp.concatenate([a, ones, b, c], axis=0)


def dot(a, b):
    return jnp.dot(a, b, preferred_element_type=F32)


def chunk_row(ref, chunks):
    return jnp.concatenate([ref[c] for c in range(chunks)], axis=1)


def peak8(scores):
    rows, cols = scores.shape
    return jnp.max(scores.reshape(rows // 8, 8, cols), axis=0)


def weighted(expos, means, k):
    high = expos.astype(BF16)
    low = (expos - high.astype(F32)).astype(BF16)
    m = means[:, k * BLOCK : (k + 1) * BLOCK]
    full, rest = dot(m, high), dot(m[:80], low)
    return [full[:48] + rest[:48], full[48:80] + full[80:112] + rest[48:80]]


def joined(sums):
    part, tail = sums
    return part[:32] + tail, part[32:40]


def forward_kernel(scale, x_ref, y_ref, g_ref, out_ref, keys, queries):
    count = y_ref.shape[1]
    y = y_ref[...]
    weight = g_ref[...] * (LOG2E / EPS) - scale * jnp.sum(y * y, axis=0, keepdims=True)
    keys[...] = key_stack(y, weight).T
    chunks = x_ref.shape[0]
    queries[...] = query_stack(chunk_row(x_ref, chunks) * (2.0 * scale), None)

    for at in range(queries.shape[1] // TILE):
        q = queries[:, at * TILE : (at + 1) * TILE]
        peak, total = None, None
        for k in range(count // SMALL):
            s = dot(keys[k * SMALL : (k + 1) * SMALL, :], q).reshape(SMALL // 8, 8, TILE)
            top = jnp.max(s, axis=0)
            later = top if peak is None else jnp.maximum(peak, top)
            t = jnp.sum(jnp.exp2(s - later[None]), axis=0)
            total = t if total is None else total * jnp.exp2(peak - later) + t
            peak = later
        top = jnp.max(peak, axis=0, keepdims=True)
        total = jnp.sum(total * jnp.exp2(peak - top), axis=0, keepdims=True)
        pair = jnp.concatenate([top, total], axis=0)
        for c in range(out_ref.shape[0]):
            out_ref[c, :, at * TILE : (at + 1) * TILE] = pair


def backward_kernel(scale, total_count, x_ref, y_ref, stats_ref, out_ref, h_ref, keys, queries, means, lse):
    chunks = x_ref.shape[0]
    x = chunk_row(x_ref, chunks)
    peaks = stats_ref[:, 0, :]
    top = jnp.max(peaks, axis=0, keepdims=True)
    total = jnp.sum(stats_ref[:, 1, :] * jnp.exp2(peaks - top), axis=0, keepdims=True)
    h = -math.log2(total_count) - (top + jnp.log2(total))
    h_ref[...] = h
    keys[...] = key_stack(x, h).T
    queries[...] = query_stack(y_ref[...] * (2.0 * scale), None)
    means[...] = mean_rows(x)

    for at in range(queries.shape[1] // TILE):
        q = queries[:, at * TILE : (at + 1) * TILE]
        peak, sums = None, None
        for k in range(keys.shape[0] // BLOCK):
            s = dot(keys[k * BLOCK : (k + 1) * BLOCK, :], q)
            top = jnp.max(peak8(s), axis=0, keepdims=True)
            later = top if peak is None else jnp.maximum(peak, top)
            part = weighted(jnp.exp2(s - later), means, k)
            if sums is None:
                sums = part
            else:
                factor = jnp.exp2(peak - later)
                sums = [old * factor + new for old, new in zip(sums, part)]
            peak = later
        mean, total = joined(sums)
        mean, total = mean / total[:1], total[:1]
        value = peak + jnp.log2(total)
        for c in range(TILE // LANES):
            cut = slice(c * LANES, (c + 1) * LANES)
            to = at * (TILE // LANES) + c
            out_ref[to, :32, :] = mean[:, cut]
            lse[to : to + 1, :] = value[:, cut]

    rows = lse[...]
    for c in range(out_ref.shape[0]):
        out_ref[c, 32:, :] = rows


def reduce_kernel(in_ref, out_ref, lse_ref):
    me = lax.axis_index("row")
    every = in_ref[:, 32:, :]
    top = jnp.max(every, axis=0)
    lse_ref[...] = top + jnp.log2(jnp.sum(jnp.exp2(every - top[None]), axis=0))
    mine = in_ref[:, pl.ds(32 + me, 1), :]
    share = jnp.exp2(mine - lse_ref[pl.ds(me, 1), :][None])
    out_ref[...] = jnp.sum(in_ref[:, :32, :] * share, axis=0)


def plan_kernel(scale, x_ref, y_ref, h_ref, lse_ref, out_ref, keys, queries, means):
    y = y_ref[...]
    lse = jnp.concatenate([lse_ref[c : c + 1, :] for c in range(lse_ref.shape[0])], axis=1)
    keys[...] = key_stack(y, -lse).T
    chunks = x_ref.shape[0]
    queries[...] = query_stack(chunk_row(x_ref, chunks) * (2.0 * scale), h_ref[...])
    means[...] = mean_rows(y)

    for at in range(queries.shape[1] // TILE):
        q = queries[:, at * TILE : (at + 1) * TILE]
        sums = None
        for k in range(keys.shape[0] // BLOCK):
            e = jnp.exp2(dot(keys[k * BLOCK : (k + 1) * BLOCK, :], q))
            part = weighted(e, means, k)
            sums = part if sums is None else [old + new for old, new in zip(sums, part)]
        mean, total = joined(sums)
        for c in range(TILE // LANES):
            cut = slice(c * LANES, (c + 1) * LANES)
            out_ref[at * (TILE // LANES) + c, :32, :] = mean[:, cut]
            out_ref[at * (TILE // LANES) + c, 32:, :] = total[:, cut]


def outward(hop, z):
    return z + hop if z % 2 == 1 else z - hop


def from_rows(value, rows, level, side):
    levels = rows // 2
    return lax.ppermute(value, "row", [(level(r // 2) % levels * 2 + (r % 2 ^ side), r) for r in range(rows)])


def potentials_kernel(scale, total_count, x_ref, y_ref, h_ref, lse_ref, f_ref, g_ref):
    x, y = chunk_row(x_ref, x_ref.shape[0]), y_ref[...]
    lse = jnp.concatenate([lse_ref[c : c + 1, :] for c in range(lse_ref.shape[0])], axis=1)
    x_sq = jnp.sum(x * x, axis=0, keepdims=True)
    y_sq = jnp.sum(y * y, axis=0, keepdims=True)
    f_ref[...] = (EPS / LOG2E) * (h_ref[...] + scale * x_sq)
    g_ref[...] = (EPS / LOG2E) * (scale * y_sq - math.log2(total_count) - lse)


def finish_kernel(in_ref, *refs):
    pieces, (out_ref, inv_ref) = refs[:-2], refs[-2:]
    sums = jnp.sum(in_ref[...], axis=0)
    out_ref[...] = sums[:32] / sums[32:33]
    me = lax.axis_index("row")
    levels = inv_ref.shape[1] // LANES // 2
    level, side = me // 2, me % 2
    sign = 2 * (level % 2) - 1
    for ref, hop in zip(pieces, (0,) + HOPS):
        source = lax.rem(level + sign * hop + levels, levels)
        mate = source + 1 - 2 * (source % 2)
        for at in range(4):
            chunk = (source if at < 2 else mate) * 2 + (side if at % 2 == 0 else 1 - side)
            inv_ref[:, pl.ds(pl.multiple_of(chunk * LANES, LANES), LANES)] = ref[at * 32 : (at + 1) * 32, :]


def call(body, outs, scratch, flops, *args):
    return pl.pallas_call(
        body,
        out_shape=[jax.ShapeDtypeStruct(s, F32) for s in outs],
        in_specs=[pl.BlockSpec(memory_space=pltpu.VMEM)] * len(args),
        out_specs=[pl.BlockSpec(memory_space=pltpu.VMEM)] * len(outs),
        scratch_shapes=scratch,
        compiler_params=pltpu.CompilerParams(vmem_limit_bytes=VMEM_LIMIT),
        cost_estimate=pl.CostEstimate(flops=flops, bytes_accessed=1 << 20, transcendentals=0),
    )(*args)


def local(source_points, target_points, target_potential):
    width, own = source_points.shape
    cols, rows = lax.axis_size("col"), lax.axis_size("row")
    n, m = own * cols, target_points.shape[1]
    source_count, target_count = n * rows, m * cols
    scale = LOG2E / (2.0 * width * EPS)
    depth = 6 * width + 16
    keys = pltpu.VMEM((m, depth), BF16)
    queries = pltpu.VMEM((depth, n), BF16)
    means = pltpu.VMEM((3 * width + 16, m), BF16)
    flops = 2 * n * m * 256

    x = lax.all_to_all(jnp.broadcast_to(source_points, (cols, width, own)), "col", 0, 0)
    (stats,) = call(
        functools.partial(forward_kernel, scale),
        [(cols, 2, n)],
        [keys, queries],
        flops,
        x,
        target_points,
        target_potential.reshape(1, m),
    )
    stats = lax.all_to_all(stats, "col", 0, 0)
    partial, h = call(
        functools.partial(backward_kernel, scale, target_count),
        [(rows, width + rows, m // rows), (1, n)],
        [keys, queries, means, pltpu.VMEM((rows, m // rows), F32)],
        2 * flops,
        x,
        target_points,
        stats,
    )
    partial = lax.all_to_all(partial, "row", 0, 0)
    inverse, lse = call(reduce_kernel, [(width, m // rows), (rows, m // rows)], [], 1 << 20, partial)
    pieces = [inverse] + [from_rows(inverse, rows, functools.partial(operator.xor, level), side) for level, side in ((0, 1), (1, 0), (1, 1))]
    four = jnp.concatenate(pieces, axis=0)
    pieces = [four] + [from_rows(four, rows, functools.partial(outward, hop), 0) for hop in HOPS]
    (plan,) = call(
        functools.partial(plan_kernel, scale),
        [(cols, width + 8, own)],
        [keys, queries, means],
        2 * flops,
        x,
        target_points,
        h,
        lse,
    )
    plan, h, lse = lax.optimization_barrier((plan, h, lse))
    plan = lax.all_to_all(plan, "col", 0, 0)
    f, g = call(
        functools.partial(potentials_kernel, scale, source_count),
        [(1, n), (1, m)],
        [],
        1 << 20,
        x,
        target_points,
        h,
        lse,
    )
    transport_map, inverse_map = call(finish_kernel, [(width, own), (width, m)], [], 1 << 20, plan, *pieces)
    return f.reshape(n), g.reshape(m), transport_map, inverse_map


def solution(mesh):
    in_specs = (P(None, ("row", "col")), P(None, "col"), P("col"))
    out_specs = (P("row"), P("col"), P(None, ("row", "col")), P(None, "col"))
    return jax.shard_map(local, mesh=mesh, in_specs=in_specs, out_specs=out_specs, check_vma=False)
```
